256 devices in a mesh: pole: 8 (over z), row: 4 (over x), col: 8 (over y, core).
Axes of the slice: x: 4, y: 4, z: 8, core: 2. Of those that a mesh axis runs over, the one named last changes fastest.
Arguments:
- green_blocks: bfloat16 [32, 8, 192, 6144], P('pole', 'col', None, 'row'), parts along dimension 0, may hold values from -0.078125 to 0.078125
- lower_panel: bfloat16 [6144, 256, 128], P(('row', 'col'), 'pole'), parts along dimension 1, may hold values from -1.5 to 1.5
- pattern: int32 [48, 32], replicated, may hold values 0 or 1
- pivot_inverse: float32 [32, 1024, 128], P(('row', 'col'), 'pole'), parts along dimension 1, may hold values from -6 to 6
Outputs:
- green_panel: bfloat16 [49152, 32, 128], P('pole', ('row', 'col')), parts along dimension 0
- green_diag: float32 [32, 1024, 128], P(('row', 'col'), 'pole'), parts along dimension 1
The draws below stay inside these ranges and needn't reach their ends.
There are 8 independent parts, one for each index of `pole`. The reference program is written for one: setup_inputs(seed, part) draws one part's arguments, and reference() takes and returns one part's arrays. A program takes and returns all parts, laid end to end along the dimension named above; an argument that names none is the same for every part. Nothing has to cross between parts.
All inputs are finite; a program needn't handle non-finite values.
Results may differ from the reference program's by a relative error of at most 0.01.
Values may be sent and summed in bfloat16 or wider, within the bound.
No kernel may reach another device: no remote copies, remote signals or barrier semaphores. Data moves between devices by JAX's collectives and lax.ppermute only.
A program may use at most 128 MiB of HBM per device.

```python
import jax
import jax.numpy as jnp
from jax import lax

BLK = 128
RDEV = 192
ORDER = 6144
NBLK = 48
NK = 32
N_ROW = 4
N_COL = 8


def place_ends(values, own_key, low, top_value):
    spot = [jax.random.randint(jax.random.fold_in(own_key, axis), (), 0, length) for axis, length in enumerate(values.shape)]
    main_axis = values.shape.index(max(values.shape))
    beside = spot[:main_axis] + [(spot[main_axis] + 1) % values.shape[main_axis]] + spot[main_axis + 1:]
    return values.at[tuple(spot)].set(low).at[tuple(beside)].set(top_value)


def with_spikes(array, own_key, source, target, blocks, factor):
    def block_of(dim):
        return (jnp.arange(array.shape[dim]) // (array.shape[dim] // blocks)).reshape((-1,) + (1,) * (array.ndim - 1 - dim))

    first = jax.random.permutation(own_key, blocks)[block_of(target)]
    far = (block_of(target) + blocks // 2) % blocks
    return jnp.where((block_of(source) == first) | (block_of(source) == far), factor * array, array)


def steps_of(own_key, shape, shards, least, top_value):
    level = 1.0
    for position, shards_of in shards:
        steps = jax.random.uniform(jax.random.fold_in(jax.random.fold_in(own_key, 6), position), (shards_of,), jnp.float32, least / len(shards), top_value / len(shards))
        level = level * jnp.repeat(jnp.exp(steps), shape[position] // shards_of).reshape((-1,) + (1,) * (len(shape) - 1 - position))
    return level


def scatter_about(key, shape, spread, reach, cuts=(), dtype=jnp.bfloat16):
    drawn = jax.random.normal(key, shape, jnp.float32) * spread
    if len(cuts) > 0:
        drawn = steps_of(key, shape, cuts, -0.22, 0.18) * drawn
    return jnp.clip(drawn, min=-reach, max=reach).astype(dtype)


def gaussian_with(rng, extent, spread, bound, cuts, heavy, kind=jnp.bfloat16):
    values = spread * jax.random.normal(rng, extent, jnp.float32)
    if cuts:
        values = values * steps_of(rng, extent, cuts, -0.22, 0.18)
    return jnp.clip(with_spikes(values, jax.random.fold_in(rng, 3), *heavy), -bound, bound).astype(kind)


def setup_inputs(seed: int = 0, part: int = 0) -> dict:
    seeds = jax.random.split(jax.random.key(seed), 5)
    own_keys = jax.random.split(jax.random.fold_in(seeds[4], part), 5)
    green_blocks = scatter_about(own_keys[0], (N_ROW, N_COL, RDEV, ORDER), ORDER ** -0.5, 0.078125, ((1, 8), (3, 4)))
    lower_panel = gaussian_with(own_keys[1], (ORDER, NK, BLK), 0.25, 1.5, ((0, 32),), (0, 1, 32, 2.75))
    pattern = place_ends((jax.random.randint(seeds[2], (NBLK, NK), 0, 2) < 1).astype(jnp.int32), jax.random.fold_in(seeds[2], 1), 0, 1)
    pivot_inverse = scatter_about(own_keys[3], (NK, BLK, BLK), 1.0, 6.0, ((0, 32),), jnp.float32)
    return dict(green_blocks=green_blocks, lower_panel=lower_panel, pattern=pattern, pivot_inverse=pivot_inverse)


def reference(green_blocks, lower_panel, pattern, pivot_inverse):
    matrix = green_blocks.reshape(ORDER, ORDER)
    row_mask = jnp.repeat(pattern, BLK, axis=0)
    masked = lower_panel * row_mask[:, :, None].astype(jnp.bfloat16)
    flat = masked.reshape(ORDER, NK * BLK)
    span = ORDER // N_ROW
    product = jnp.zeros((ORDER, NK * BLK), jnp.float32)
    for index in range(N_ROW):
        piece = jnp.dot(matrix[:, index * span:(index + 1) * span], flat[index * span:(index + 1) * span], preferred_element_type=jnp.float32)
        rounded = lax.optimization_barrier(piece.astype(jnp.bfloat16))
        product = product + rounded.astype(jnp.float32)
    resolved = product.reshape(ORDER, NK, BLK)
    green_panel = (-(resolved * row_mask[:, :, None].astype(jnp.float32))).astype(jnp.bfloat16)
    green_diag = pivot_inverse + jnp.einsum("rkb,rkc->kbc", masked.astype(jnp.float32), resolved, precision=lax.Precision.HIGHEST)
    return green_panel, green_diag
```

```python
import functools

import jax
import jax.numpy as jnp
from jax import lax
from jax.experimental import pallas as pl
from jax.experimental.pallas import tpu as pltpu
from jax.sharding import PartitionSpec as P

BF16 = jnp.bfloat16
F32 = jnp.float32
SMEM = pl.BlockSpec(memory_space=pltpu.SMEM)
VMEM = pl.BlockSpec(memory_space=pltpu.VMEM)
ANY = pl.BlockSpec(memory_space=pl.ANY)

W = 128
RD = 192
CH = 2 * RD
NR = 4
NY = 4
SPAN = NY * CH
HALF = NR * RD
ORDER = NR * NY * CH
PARAMS = pltpu.CompilerParams(vmem_limit_bytes=40 * 1024 * 1024)


def run_copies(copies):
    for copy in copies:
        copy.start()
    for copy in copies:
        copy.wait()


def group_of(r, s, q):
    return lax.rem(r + 3 - s, 4) if q < 2 else lax.rem(r + 1 + s, 4)


def prep_kernel(place, pattern, panel, mine0, theirs0, mine, theirs):
    r, k, position = place[0], place[2], place[3]
    for s in range(NR):
        for q in range(NY):
            for parity, (first, rest) in ((k, (mine0, mine)), (1 - k, (theirs0, theirs))):
                number = group_of(r, s, q) * 8 + q * 2 + parity
                for part in range(3):
                    block = lax.div(position * 3 + part, 2)
                    keep = pattern[block, number].astype(F32)
                    rows = pl.ds(part * 64, 64)
                    value = (panel[number, rows, :].astype(F32) * keep).astype(BF16)
                    if s == 0:
                        first[q, rows, :] = value
                    else:
                        rest[s - 1, q, rows, :] = value


def first_chunk_kernel(place, mine, got, chunk, sems):
    k = place[2]
    run_copies(
        [
            pltpu.make_async_copy(source, chunk.at[:, half], sems.at[i])
            for i, (source, half) in enumerate(((mine, k), (got, 1 - k)))
        ]
    )


def chunks_kernel(place, mine0, got0, mine, got, c1, c2, c3, x1, x3, sems):
    k = place[2]
    copies = []
    for first, rest, half in ((mine0, mine, k), (got0, got, 1 - k)):
        moves = [
            (rest.at[0], c1.at[:, half]),
            (rest.at[1], c2.at[:, half]),
            (rest.at[2], c3.at[:, half]),
            (rest.at[1, 0:2], x1.at[0:2, half]),
            (first.at[2:4], x1.at[2:4, half]),
            (first.at[0:2], x3.at[0:2, half]),
            (rest.at[1, 2:4], x3.at[2:4, half]),
        ]
        for source, target in moves:
            copies.append(pltpu.make_async_copy(source, target, sems.at[len(copies)]))
    run_copies(copies)


def product_kernel(summed, last, place, green, own, below, above, far_a, far_b, *rest):
    rest = list(rest)
    acc = [rest.pop(0), rest.pop(0)] if summed else None
    outs = [rest.pop(0) for _ in range(4 if last else 2)]
    panel, sems = rest[:2]
    y = place[1]

    def at(step, part):
        rows = pl.ds(pl.multiple_of(lax.rem(y + step, 4) * CH, CH), CH)
        return panel.at[part, rows, :]

    everything = slice(0, 4)
    run_copies(
        [
            pltpu.make_async_copy(source, at(step, part), sems.at[i])
            for i, (source, step, part) in enumerate(
                (
                    (own, 0, everything),
                    (below, 3, everything),
                    (above, 1, everything),
                    (far_a, 2, slice(0, 2)),
                    (far_b, 2, slice(2, 4)),
                )
            )
        ]
    )
    for h in range(2):
        both = jnp.concatenate([panel[2 * h], panel[2 * h + 1]], axis=1)
        value = jnp.dot(green[...], both, preferred_element_type=F32)
        for i in range(2):
            part = value[:, i * W : (i + 1) * W]
            if summed:
                part = part + acc[h][i].astype(F32)
            if last:
                rest[2][2 * h + i] = part.astype(BF16)
            else:
                outs[h][i] = part.astype(BF16)
    if last:
        run_copies(
            [
                pltpu.make_async_copy(rest[2].at[lax.rem(y + d, 4)], outs[d], sems.at[d])
                for d in range(4)
            ]
        )


def product(place, green, pieces, acc, last):
    flat = [p.reshape(p.shape[0], CH, W) for p in pieces]
    if last:
        out_shape = [jax.ShapeDtypeStruct((HALF, W), BF16)] * 4
    else:
        out_shape = [jax.ShapeDtypeStruct((2, HALF, W), BF16)] * 2
    scratch = [pltpu.VMEM((4, SPAN, W), BF16), pltpu.SemaphoreType.DMA((5,))]
    if last:
        scratch.append(pltpu.VMEM((4, HALF, W), BF16))
    return pl.pallas_call(
        functools.partial(product_kernel, bool(acc), last),
        out_shape=out_shape,
        in_specs=[SMEM, VMEM] + [ANY] * 5 + [VMEM] * len(acc),
        out_specs=[ANY] * 4 if last else [VMEM] * 2,
        scratch_shapes=scratch,
        compiler_params=PARAMS,
        cost_estimate=pl.CostEstimate(
            flops=2 * HALF * SPAN * 4 * W, bytes_accessed=8 * 2**20, transcendentals=0
        ),
    )(place, green, *flat, *acc)


def turn_kernel(place, x0, x1, x2, x3, t0, t1, t2, t3, sems):
    y = place[1]
    copies = []
    for e, target in enumerate((t0, t1, t2, t3)):
        for d, source in enumerate((x0, x1, x2, x3)):
            copies.append(
                pltpu.make_async_copy(
                    source.at[lax.rem(y + e, 4)], target.at[d], sems.at[len(copies)]
                )
            )
    run_copies(copies)


def column_kernel(place, t0, t1, t2, t3, out, column, sems):
    r, y = place[0], place[1]
    copies = []
    for e, source in enumerate((t0, t1, t2, t3)):
        for d in range(4):
            index = lax.rem(r + 4 - d, 4) * 4 + lax.rem(y + 4 - e, 4)
            rows = pl.ds(pl.multiple_of(index * CH, CH), CH)
            copies.append(
                pltpu.make_async_copy(source.at[d], column.at[rows], sems.at[len(copies)])
            )
    run_copies(copies)
    out[...] = column[...].T


def final_kernel(place, pattern, pivot, column_t, *rest):
    parts, (panel, diag, resolved, sems) = rest[:8], rest[8:]
    y, k, position = place[1], place[2], place[3]
    copies = []
    for half in range(2):
        parity = k if half == 0 else 1 - k
        for d in range(4):
            c = lax.rem(y + 4 - d, 4) * 2 + parity
            for j in range(4):
                rows = pl.ds(pl.multiple_of((j * 8 + c) * RD, RD), RD)
                copies.append(
                    pltpu.make_async_copy(
                        parts[half * 4 + d].at[j * RD : (j + 1) * RD],
                        resolved.at[rows],
                        sems.at[len(copies)],
                    )
                )
    run_copies(copies)
    diag[...] = pivot[...] + jnp.dot(column_t[...], resolved[...], preferred_element_type=F32)
    for block in range(ORDER // W):
        keep = pattern[block, position].astype(F32)
        rows = pl.ds(block * W, W)
        panel[rows, :] = (-(resolved[rows, :].astype(F32) * keep)).astype(BF16)


def local(green_blocks, lower_panel, pattern, pivot_inverse):
    r = lax.axis_index("row")
    col = lax.axis_index("col")
    place = jnp.stack([r, col // 2, col % 2, r * 8 + col]).astype(jnp.int32)

    def sib(v):
        return lax.ppermute(v, "col", [(c, c ^ 1) for c in range(8)])

    def over_y(v, d):
        return lax.ppermute(v, "col", [(c, (c + 2 * d) % 8) for c in range(8)])

    def over_x(v, d):
        return lax.ppermute(v, "row", [(i, (i + d) % 4) for i in range(4)])

    def call(kernel, outs, ins, specs, out_spec=VMEM, scratch=(), bytes_accessed=4 * 2**20):
        return pl.pallas_call(
            kernel,
            out_shape=[jax.ShapeDtypeStruct(s, d) for s, d in outs],
            in_specs=specs,
            out_specs=[out_spec] * len(outs),
            scratch_shapes=list(scratch),
            compiler_params=PARAMS,
            cost_estimate=pl.CostEstimate(
                flops=0, bytes_accessed=bytes_accessed, transcendentals=0
            ),
        )(*ins)

    panel = lower_panel.transpose(1, 0, 2)
    small, large = ((4, RD, W), BF16), ((3, 4, RD, W), BF16)
    mine0, theirs0, mine, theirs = call(
        prep_kernel,
        [small, small, large, large],
        (place, pattern, panel),
        [SMEM, SMEM, VMEM],
    )
    got0 = sib(theirs0)
    got = sib(theirs)
    green_own = green_blocks.reshape(HALF, SPAN)
    green_sib = sib(green_own)

    dma = pltpu.SemaphoreType.DMA
    chunk = ((4, 2, RD, W), BF16)
    (chunk0,) = call(
        first_chunk_kernel, [chunk], (place, mine0, got0), [SMEM, ANY, ANY], ANY, [dma((2,))]
    )
    chunk1, chunk2, chunk3, x1, x3 = call(
        chunks_kernel,
        [chunk] * 5,
        (place, mine0, got0, mine, got),
        [SMEM] + [ANY] * 4,
        ANY,
        [dma((14,))],
    )
    chunks = [chunk0, chunk1, chunk2, chunk3]
    pieces = []
    for own in chunks:
        below, above = over_y(own, 1), over_y(own, -1)
        far_a, far_b = over_y(below[0:2], 1), over_y(above[2:4], -1)
        pieces.append((own, below, above, far_a, far_b))

    columns = [chunk3, over_x(x1, 1), over_x(chunk1, 2), over_x(x3, 3)]

    parts = []
    greens = (green_own, green_sib)
    acc = [(), ()]
    for s in range(NR):
        for half in range(2):
            out = product(place, greens[half], pieces[s], acc[half], s == NR - 1)
            if s < NR - 1:
                acc[half] = (over_x(out[0], 1), over_x(out[1], -1))
            else:
                parts += [out[0]] + [over_y(out[d], d) for d in (1, 2, 3)]

    turned = call(
        turn_kernel,
        [((4, CH, W), BF16)] * 4,
        (place, *[c.reshape(4, CH, W) for c in columns]),
        [SMEM] + [ANY] * 4,
        ANY,
        [dma((16,))],
    )
    turned = [turned[0]] + [over_y(turned[e], e) for e in (1, 2, 3)]
    (column_t,) = call(
        column_kernel,
        [((W, ORDER), BF16)],
        (place, *turned),
        [SMEM] + [ANY] * 4,
        VMEM,
        [pltpu.VMEM((ORDER, W), BF16), dma((16,))],
    )
    green_panel, green_diag = call(
        final_kernel,
        [((ORDER, W), BF16), ((W, W), F32)],
        (place, pattern, pivot_inverse.reshape(W, W), column_t, *parts),
        [SMEM, SMEM, VMEM, VMEM] + [ANY] * 8,
        VMEM,
        [pltpu.VMEM((ORDER, W), BF16), dma((32,))],
    )
    return green_panel.reshape(ORDER, 1, W), green_diag.reshape(1, W, W)


def solution(mesh):
    placed = (
        P("pole", "col", None, "row"),
        P(("row", "col"), "pole", None),
        P(),
        P(("row", "col"), "pole", None),
    )
    return jax.shard_map(
        local,
        mesh=mesh,
        in_specs=placed,
        out_specs=(P("pole", ("row", "col"), None), P(("row", "col"), "pole", None)),
        check_vma=False,
    )
```

```python
import functools

import jax
import jax.numpy as jnp
from jax import lax
from jax.experimental import pallas as pl
from jax.experimental.pallas import tpu as pltpu
from jax.sharding import PartitionSpec as P

BF16 = jnp.bfloat16
F32 = jnp.float32
SMEM = pl.BlockSpec(memory_space=pltpu.SMEM)
VMEM = pl.BlockSpec(memory_space=pltpu.VMEM)
ANY = pl.BlockSpec(memory_space=pl.ANY)

W = 128
RD = 192
CH = 2 * RD
NR = 4
NY = 4
NC = 8
SPAN = NC * RD
HALF = NR * RD
ORDER = NR * NC * RD


def run_copies(copies):
    for copy in copies:
        copy.start()
    for copy in copies:
        copy.wait()


def call(kernel, outs, ins, specs, out_specs, scratch=(), flops=0, bytes_accessed=4 * 2**20):
    return pl.pallas_call(
        kernel,
        out_shape=[jax.ShapeDtypeStruct(s, d) for s, d in outs],
        in_specs=specs,
        out_specs=out_specs,
        scratch_shapes=list(scratch),
        compiler_params=pltpu.CompilerParams(vmem_limit_bytes=24 * 1024 * 1024),
        cost_estimate=pl.CostEstimate(
            flops=flops, bytes_accessed=bytes_accessed, transcendentals=0
        ),
    )(*ins)


def group_of(r, s, q):
    return lax.rem(r + 3 - s, 4) if q < 2 else lax.rem(r + 1 + s, 4)


def prep_kernel(place, pattern, panel, mine0, theirs0, mine, theirs, turned, sems):
    r, k, position = place[0], place[2], place[3]
    for group in range(NR):
        for part in range(3):
            block = lax.div(position * 3 + part, 2)
            for piece in range(2):
                rows = pl.ds(part * 64 + piece * 32, 32)
                value = jnp.swapaxes(
                    panel[rows, group * 8 : group * 8 + 8, :].astype(F32), 0, 1
                )
                for q in range(NY):
                    s = lax.rem(r + 3 - group, 4) if q < 2 else lax.rem(group + 3 - r, 4)
                    for parity in range(2):
                        keep = pattern[group * 8 + q * 2 + parity, block].astype(F32)
                        turned[lax.rem(parity + k, 2), s, q, rows, :] = (
                            value[q * 2 + parity] * keep
                        ).astype(BF16)
    run_copies(
        [
            pltpu.make_async_copy(turned.at[who, part], out, sems.at[i])
            for i, (who, part, out) in enumerate(
                (
                    (1, 0, theirs0),
                    (0, 0, mine0),
                    (1, slice(1, 4), theirs),
                    (0, slice(1, 4), mine),
                )
            )
        ]
    )


def first_chunk_kernel(place, mine, got, *rest):
    chunk, sems = rest[-2:]
    k = place[2]
    run_copies(
        [
            pltpu.make_async_copy(source, chunk.at[:, half], sems.at[i])
            for i, (source, half) in enumerate(((mine, k), (got, 1 - k)))
        ]
    )


def chunks_kernel(place, mine0, got0, mine, got, after, c1, c2, c3, x1, x3, sems):
    k = place[2]
    copies = []
    for first, rest, half in ((mine0, mine, k), (got0, got, 1 - k)):
        moves = [
            (rest.at[0], c1.at[:, half]),
            (rest.at[1], c2.at[:, half]),
            (rest.at[2], c3.at[:, half]),
            (rest.at[1, 0:2], x1.at[0:2, half]),
            (first.at[2:4], x1.at[2:4, half]),
            (first.at[0:2], x3.at[0:2, half]),
            (rest.at[1, 2:4], x3.at[2:4, half]),
        ]
        for source, target in moves:
            copies.append(pltpu.make_async_copy(source, target, sems.at[len(copies)]))
    run_copies(copies)


def after_kernel(value, *rest):
    out, sems = rest[-2:]
    run_copies([pltpu.make_async_copy(value, out, sems.at[0])])


def load_panel(y, pieces, panel, sems):
    own, below, above, far_a, far_b = pieces

    def at(step, part):
        rows = pl.ds(pl.multiple_of(lax.rem(y + step, 4) * CH, CH), CH)
        return panel.at[part, rows, :]

    everything = slice(0, 4)
    run_copies(
        [
            pltpu.make_async_copy(source, at(step, part), sems.at[i])
            for i, (source, step, part) in enumerate(
                (
                    (own, 0, everything),
                    (below, 3, everything),
                    (above, 1, everything),
                    (far_a, 2, slice(0, 2)),
                    (far_b, 2, slice(2, 4)),
                )
            )
        ]
    )


def product_kernel(summed, place, green, *rest):
    pieces, rest = rest[:5], rest[5:]
    acc, (out0, out1, panel, sems) = rest[: 2 * summed], rest[-4:]
    load_panel(place[1], pieces, panel, sems)
    for h, out in enumerate((out0, out1)):
        both = jnp.concatenate([panel[2 * h], panel[2 * h + 1]], axis=1)
        value = jnp.dot(green[...], both, preferred_element_type=F32)
        for i in range(2):
            part = value[:, i * W : (i + 1) * W]
            if summed:
                part = part + acc[h][i].astype(F32)
            out[i] = part.astype(BF16)


def product(place, green, pieces, acc, after=()):
    return call(
        functools.partial(product_kernel, int(bool(acc))),
        [((2, HALF, W), BF16)] * 2,
        (place, green, *pieces, *acc, *after),
        [SMEM, VMEM] + [ANY] * 5 + [VMEM] * len(acc) + [ANY] * len(after),
        [VMEM] * 2,
        [pltpu.VMEM((4, SPAN, W), BF16), pltpu.SemaphoreType.DMA((5,))],
        flops=2 * HALF * SPAN * 4 * W,
    )


def last_kernel(half, place, pattern, green, *rest):
    pieces, acc, outs, (panel, sems) = rest[:5], rest[5:7], rest[7:11], rest[11:]
    r, y, k = place[0], place[1], place[2]
    load_panel(y, pieces, panel, sems)
    c = y * 2 + (k if half == 0 else 1 - k)
    for h in range(2):
        order = [lax.rem(y + 2 * h + i, 4) for i in range(2)]
        both = jnp.concatenate([panel[order[0]], panel[order[1]]], axis=1)
        value = jnp.dot(green[...], both, preferred_element_type=F32)
        for i, q in enumerate(order):
            number = r * 8 + q * 2 + k
            for j in range(NR):
                for piece in range(3):
                    keep = -pattern[number, lax.div((j * 8 + c) * 3 + piece, 2)].astype(F32)
                    start = j * RD + piece * 64
                    rows = slice(start, start + 64)
                    before = jnp.where(
                        q < 2, acc[0][lax.rem(q, 2), rows, :], acc[1][lax.rem(q, 2), rows, :]
                    )
                    part = value[rows, i * W : (i + 1) * W] + before.astype(F32)
                    outs[2 * h + i][j, piece * 64 : piece * 64 + 64, :] = (part * keep).astype(BF16)


def columns_kernel(place, x0, x1, x2, x3, out, columns, sems):
    r, k = place[0], place[2]
    run_copies(
        [
            pltpu.make_async_copy(source, columns.at[lax.rem(r + 4 - d, 4)], sems.at[d])
            for d, source in enumerate((x0, x1, x2, x3))
        ]
    )
    for half in range(2):
        parity = k if half == 0 else 1 - k
        for q in range(NY):
            out[half, q] = columns[:, q, parity].reshape(HALF, W).T


def diag_kernel(place, columns_t, *rest):
    ended, outs = rest[:8], rest[8:]
    y = place[1]
    for d in range(4):
        q = lax.rem(y + d, 4)
        total = jnp.zeros((W, W), F32)
        for half in range(2):
            total += jnp.dot(
                columns_t[half, q],
                ended[half * 4 + d][...].reshape(HALF, W),
                preferred_element_type=F32,
            )
        outs[d][...] = -total


def final_kernel(place, pivot, *rest):
    terms, parts, (panel, diag, sems) = rest[:4], rest[4:12], rest[12:]
    y, k = place[1], place[2]
    copies = []
    for half in range(2):
        for d in range(4):
            c = lax.rem(y + 4 - d, 4) * 2 + (k if half == 0 else 1 - k)
            copies.append(
                pltpu.make_async_copy(
                    parts[half * 4 + d], panel.at[:, c], sems.at[len(copies)]
                )
            )
    for copy in copies:
        copy.start()
    diag[...] = pivot[...] + ((terms[0][...] + terms[1][...]) + (terms[2][...] + terms[3][...]))
    for copy in copies:
        copy.wait()


def local(green_blocks, lower_panel, pattern, pivot_inverse):
    r = lax.axis_index("row")
    col = lax.axis_index("col")
    place = jnp.stack([r, col // 2, col % 2, r * 8 + col]).astype(jnp.int32)
    dma = pltpu.SemaphoreType.DMA

    def sib(v):
        return lax.ppermute(v, "col", [(c, c ^ 1) for c in range(8)])

    def over_y(v, d):
        return lax.ppermute(v, "col", [(c, (c + 2 * d) % 8) for c in range(8)])

    def over_x(v, d):
        return lax.ppermute(v, "row", [(i, (i + d) % 4) for i in range(4)])

    pattern = pattern.T
    small, large = ((NY, RD, W), BF16), ((3, NY, RD, W), BF16)
    mine0, theirs0, mine, theirs = call(
        prep_kernel,
        [small, small, large, large],
        (place, pattern, lower_panel),
        [SMEM, SMEM, VMEM],
        [ANY] * 4,
        [pltpu.VMEM((2, NR, NY, RD, W), BF16), dma((4,))],
    )
    got0 = sib(theirs0)
    got = sib(theirs)
    green_own = green_blocks.reshape(HALF, SPAN)
    greens = (green_own, sib(green_own))

    chunk = ((NY, 2, RD, W), BF16)
    (chunk0,) = call(
        first_chunk_kernel, [chunk], (place, mine0, got0, greens[1]), [SMEM, ANY, ANY, ANY], [ANY], [dma((2,))]
    )
    chunk1, chunk2, chunk3, x1, x3 = call(
        chunks_kernel,
        [chunk] * 5,
        (place, mine0, got0, mine, got, chunk0),
        [SMEM] + [ANY] * 5,
        [ANY] * 5,
        [dma((14,))],
    )

    def put_after(value, *others):
        (out,) = call(
            after_kernel,
            [(value.shape, value.dtype)],
            (value, *others),
            [ANY] * (1 + len(others)),
            [ANY],
            [dma((1,))],
        )
        return out

    columns = [over_x(x1, 1), over_x(chunk1, 2), over_x(x3, 3)]
    (columns_t,) = call(
        columns_kernel,
        [((2, NY, W, HALF), BF16)],
        (place, chunk3, *columns),
        [SMEM] + [ANY] * 4,
        [VMEM],
        [pltpu.VMEM((NR, NY, 2, RD, W), BF16), dma((4,))],
    )

    pieces, after = [], tuple(columns)
    for own in (chunk0, chunk1, chunk2, chunk3):
        own = own.reshape(NY, CH, W)
        sent = put_after(own, *after) if pieces else own
        below, above = over_y(sent, 1), over_y(sent, -1)
        after = (below, above) if pieces else after
        far_a, far_b = over_y(below[0:2], 1), over_y(above[2:4], -1)
        pieces.append((own, below, above, far_a, far_b))

    acc = [(), ()]
    for s in range(NR - 1):
        for half in range(2):
            first = (columns_t,) if s == 0 and half == 0 else ()
            out = product(place, greens[half], pieces[s], acc[half], first)
            acc[half] = (over_x(out[0], 1), over_x(out[1], -1))
    ended, parts = [], []
    for half in range(2):
        outs = call(
            functools.partial(last_kernel, half),
            [((NR, RD, W), BF16)] * 4,
            (place, pattern, greens[half], *pieces[3], *acc[half]),
            [SMEM, SMEM, VMEM] + [ANY] * 5 + [VMEM] * 2,
            [VMEM] * 4,
            [pltpu.VMEM((4, SPAN, W), BF16), dma((5,))],
            flops=2 * HALF * SPAN * 4 * W,
        )
        ended += outs
        parts += [outs[0]] + [over_y(outs[d], d) for d in (1, 2, 3)]
    terms = call(
        diag_kernel,
        [((W, W), F32)] * 4,
        (place, columns_t, *ended),
        [SMEM] + [VMEM] * 9,
        [VMEM] * 4,
        flops=4 * ORDER * W * W,
    )
    terms = [terms[0]] + [over_y(terms[d], d) for d in (1, 2, 3)]
    green_panel, green_diag = call(
        final_kernel,
        [((NR, NC, RD, W), BF16), ((W, W), F32)],
        (place, pivot_inverse.reshape(W, W), *terms, *parts),
        [SMEM] + [VMEM] * 5 + [ANY] * 8,
        [ANY, VMEM],
        [dma((8,))],
    )
    return green_panel.reshape(ORDER, 1, W), green_diag.reshape(1, W, W)


def solution(mesh):
    placed = (
        P("pole", "col", None, "row"),
        P(("row", "col"), "pole", None),
        P(),
        P(("row", "col"), "pole", None),
    )
    return jax.shard_map(
        local,
        mesh=mesh,
        in_specs=placed,
        out_specs=(P("pole", ("row", "col"), None), P(("row", "col"), "pole", None)),
        check_vma=False,
    )
```

```python
import functools

import jax
import jax.numpy as jnp
from jax import lax
from jax.experimental import pallas as pl
from jax.experimental.pallas import tpu as pltpu
from jax.sharding import PartitionSpec as P

BF16 = jnp.bfloat16
F32 = jnp.float32
SMEM = pl.BlockSpec(memory_space=pltpu.SMEM)
VMEM = pl.BlockSpec(memory_space=pltpu.VMEM)
ANY = pl.BlockSpec(memory_space=pl.ANY)

W = 128
RD = 192
CH = 2 * RD
NR = 4
NY = 4
NC = 8
SPAN = NC * RD
HALF = NR * RD
ORDER = NR * NC * RD


def run_copies(copies):
    for copy in copies:
        copy.start()
    for copy in copies:
        copy.wait()


def call(
    kernel, outs, ins, specs, out_specs, scratch=(), flops=0, bytes_accessed=4 * 2**20, aliases=()
):
    return pl.pallas_call(
        kernel,
        out_shape=[jax.ShapeDtypeStruct(s, d) for s, d in outs],
        in_specs=specs,
        out_specs=out_specs,
        scratch_shapes=list(scratch),
        input_output_aliases=dict(aliases),
        compiler_params=pltpu.CompilerParams(vmem_limit_bytes=24 * 1024 * 1024),
        cost_estimate=pl.CostEstimate(
            flops=flops, bytes_accessed=bytes_accessed, transcendentals=0
        ),
    )(*ins)


def step_of(r, group, core):
    return lax.rem(r + 3 - group, 4) if core == 0 else lax.rem(group + 3 - r, 4)


def along(index, count, core):
    return lax.rem(index + jnp.where(core == 0, count, 4 - count), 4)


def prep_kernel(place, pattern, panel, mine0, theirs0, mine, theirs, turned, sems):
    r, k, position = place[0], place[2], place[3]
    for group in range(NR):
        for part in range(3):
            block = lax.div(position * 3 + part, 2)
            for piece in range(2):
                rows = pl.ds(part * 64 + piece * 32, 32)
                value = jnp.swapaxes(
                    panel[rows, group * 8 : group * 8 + 8, :].astype(F32), 0, 1
                )
                for q in range(NY):
                    for parity in range(2):
                        keep = pattern[group * 8 + q * 2 + parity, block].astype(F32)
                        turned[lax.rem(parity + k, 2), step_of(r, group, parity), q, rows, :] = (
                            value[q * 2 + parity] * keep
                        ).astype(BF16)
    run_copies(
        [
            pltpu.make_async_copy(turned.at[who, part], out, sems.at[i])
            for i, (who, part, out) in enumerate(
                (
                    (1, 0, theirs0),
                    (0, 0, mine0),
                    (1, slice(1, 4), theirs),
                    (0, slice(1, 4), mine),
                )
            )
        ]
    )


def first_chunk_kernel(place, mine, got, after, first, second, sems):
    k = place[2]
    copies = []
    for i, part in enumerate((first, second)):
        for source, half in ((mine, k), (got, 1 - k)):
            copies.append(
                pltpu.make_async_copy(
                    source.at[2 * i : 2 * i + 2], part.at[:, half], sems.at[len(copies)]
                )
            )
    run_copies(copies)


def chunks_kernel(place, mine0, got0, mine, got, after, c0, c1, c2, c3, sems):
    k = place[2]
    copies = []
    for first, rest, half in ((mine0, mine, k), (got0, got, 1 - k)):
        for source, chunk in ((first, c0), (rest.at[0], c1), (rest.at[1], c2), (rest.at[2], c3)):
            copies.append(
                pltpu.make_async_copy(source, chunk.at[:, half], sems.at[len(copies)])
            )
    run_copies(copies)


def load_panel(place, pieces, panel, sems):
    y, k = place[1], place[2]
    parts = len(pieces) // NY
    copies = []
    for i, source in enumerate(pieces):
        hop, part = i // parts, i % parts
        rows = pl.ds(pl.multiple_of(along(y, 4 - hop, k) * CH, CH), CH)
        numbers = slice(part * (NY // parts), (part + 1) * (NY // parts))
        copies.append(pltpu.make_async_copy(source, panel.at[numbers, rows, :], sems.at[i]))
    run_copies(copies)


def product_kernel(count, summed, place, green, *rest):
    pieces, rest = rest[:count], rest[count:]
    acc, (out, panel, sems) = rest[:summed], rest[-3:]
    load_panel(place, pieces, panel, sems)
    for h in range(2):
        both = jnp.concatenate([panel[2 * h], panel[2 * h + 1]], axis=1)
        value = jnp.dot(green[...], both, preferred_element_type=F32)
        for i in range(2):
            part = value[:, i * W : (i + 1) * W]
            if summed:
                part = part + acc[0][2 * h + i].astype(F32)
            out[2 * h + i] = part.astype(BF16)


def product(place, green, pieces, acc, after=()):
    (out,) = call(
        functools.partial(product_kernel, len(pieces), len(acc)),
        [((NY, HALF, W), BF16)],
        (place, green, *pieces, *acc, *after),
        [SMEM, VMEM] + [ANY] * len(pieces) + [VMEM] * len(acc) + [ANY] * len(after),
        [VMEM],
        [pltpu.VMEM((NY, SPAN, W), BF16), pltpu.SemaphoreType.DMA((len(pieces),))],
        flops=2 * HALF * SPAN * 4 * W,
    )
    return out


def last_kernel(half, place, pattern, green, *rest):
    pieces, acc, rest = rest[:4], rest[4], rest[5:]
    if half:
        columns_t, terms, rest = rest[0], rest[1], rest[2:]
    outs, (panel, sems) = rest[:4], rest[4:]
    r, y, k = place[0], place[1], place[2]
    load_panel(place, pieces, panel, sems)
    c = y * 2 + (k if half == 0 else 1 - k)
    for h in range(2):
        order = [lax.rem(y + 2 * h + i, 4) for i in range(2)]
        both = jnp.concatenate([panel[order[0]], panel[order[1]]], axis=1)
        value = jnp.dot(green[...], both, preferred_element_type=F32)
        for i, q in enumerate(order):
            number = r * 8 + q * 2 + k
            out = outs[2 * h + i]
            for j in range(NR):
                for piece in range(3):
                    keep = -pattern[number, lax.div((j * 8 + c) * 3 + piece, 2)].astype(F32)
                    start = j * RD + piece * 64
                    rows = slice(start, start + 64)
                    part = value[rows, i * W : (i + 1) * W] + acc[q, rows, :].astype(F32)
                    out[rows, :] = (part * keep).astype(BF16)
            if half:
                term = jnp.dot(columns_t[1, q], out[0:HALF, :], preferred_element_type=F32)
                out[HALF : HALF + W, :] = (terms[2 * h + i] - term).astype(BF16)


def diag_kernel(place, columns_t, *rest):
    ended, out = rest[:4], rest[4]
    y = place[1]
    for d in range(4):
        q = lax.rem(y + d, 4)
        out[d] = -jnp.dot(columns_t[0, q], ended[d][...], preferred_element_type=F32)


def columns_kernel(place, x0, x1, x2, x3, out, columns, sems):
    r, k = place[0], place[2]
    run_copies(
        [
            pltpu.make_async_copy(source, columns.at[along(r, 1 + s, k)], sems.at[s])
            for s, source in enumerate((x0, x1, x2, x3))
        ]
    )
    for half in range(2):
        parity = k if half == 0 else 1 - k
        for q in range(NY):
            out[half, q] = columns[:, q, parity].reshape(HALF, W).T


def final_kernel(half, place, *rest):
    if half:
        pivot, parts, (_, panel, diag, terms, sems) = rest[0], rest[1:5], rest[5:]
    else:
        parts, (panel, sems) = rest[:4], rest[4:]
    y, k = place[1], place[2]
    copies, last = [], []
    for d in range(4):
        c = lax.rem(y + 4 - d, 4) * 2 + (k if half == 0 else 1 - k)
        for j in range(NR):
            copies.append(
                pltpu.make_async_copy(
                    parts[d].at[j * RD : (j + 1) * RD], panel.at[j, c], sems.at[len(copies)]
                )
            )
        if half:
            last.append(
                pltpu.make_async_copy(
                    parts[d].at[HALF : HALF + W], terms.at[d], sems.at[NR * NY + d]
                )
            )
    for copy in last + copies:
        copy.start()
    for copy in last:
        copy.wait()
    if half:
        total = pivot[...]
        for d in range(4):
            total += terms[d].astype(F32)
        diag[...] = total
    for copy in copies:
        copy.wait()


def local(green_blocks, lower_panel, pattern, pivot_inverse):
    r = lax.axis_index("row")
    col = lax.axis_index("col")
    place = jnp.stack([r, col // 2, col % 2, r * 8 + col]).astype(jnp.int32)
    dma = pltpu.SemaphoreType.DMA

    def sib(v):
        return lax.ppermute(v, "col", [(c, c ^ 1) for c in range(8)])

    def over_y(v, d):
        return lax.ppermute(v, "col", [(c, (c + 2 * d) % 8) for c in range(8)])

    def ring_y(v):
        return lax.ppermute(v, "col", [(c, (c + (6 if c % 2 else 2)) % 8) for c in range(8)])

    def ring_x(v, d=1):
        pairs = [(i, (i + (-8 * d if i % 2 else 8 * d)) % 32) for i in range(32)]
        return lax.ppermute(v, ("row", "col"), pairs)

    pattern = pattern.T
    small, large = ((NY, RD, W), BF16), ((3, NY, RD, W), BF16)
    mine0, theirs0, mine, theirs = call(
        prep_kernel,
        [small, small, large, large],
        (place, pattern, lower_panel),
        [SMEM, SMEM, VMEM],
        [ANY] * 4,
        [pltpu.VMEM((2, NR, NY, RD, W), BF16), dma((4,))],
    )
    got0 = sib(theirs0)
    got = sib(theirs)
    green_own = green_blocks.reshape(HALF, SPAN)
    greens = (green_own, sib(green_own))

    chunk = ((NY, 2, RD, W), BF16)
    first = call(
        first_chunk_kernel,
        [((2, 2, RD, W), BF16)] * 2,
        (place, mine0, got0, greens[1]),
        [SMEM] + [ANY] * 3,
        [ANY] * 2,
        [dma((4,))],
    )
    chunks = call(
        chunks_kernel,
        [chunk] * 4,
        (place, mine0, got0, mine, got, first[0]),
        [SMEM] + [ANY] * 5,
        [ANY] * 4,
        [dma((8,))],
    )
    columns = [ring_x(chunks[s], 3 - s) for s in range(NR - 1)] + [chunks[3]]
    (columns_t,) = call(
        columns_kernel,
        [((2, NY, W, HALF), BF16)],
        (place, *columns),
        [SMEM] + [ANY] * 4,
        [VMEM],
        [pltpu.VMEM((NR, NY, 2, RD, W), BF16), dma((4,))],
    )

    pieces = []
    for parts in (first, *((c,) for c in chunks[1:])):
        held = [p.reshape(-1, CH, W) for p in parts]
        pieces.append(list(held))
        for hop in range(NY - 1):
            held = [ring_y(p) for p in held]
            pieces[-1] += held

    acc = [(), ()]
    for s in range(NR - 1):
        for half in range(2):
            after = () if s else (out,) if half else (columns_t,)
            out = product(place, greens[half], pieces[s], acc[half], after)
            acc[half] = (ring_x(out),)
    parts, terms = [], ()
    for half in range(2):
        outs = call(
            functools.partial(last_kernel, half),
            [((HALF + W * half, W), BF16)] * 4,
            (place, pattern, greens[half], *pieces[3], *acc[half], *terms),
            [SMEM, SMEM, VMEM] + [ANY] * 4 + [VMEM] * (1 + len(terms)),
            [VMEM] * 4,
            [pltpu.VMEM((NY, SPAN, W), BF16), dma((4,))],
            flops=2 * HALF * SPAN * 4 * W,
        )
        parts += [outs[0]] + [over_y(outs[d], d) for d in (1, 2, 3)]
        if half == 0:
            (term,) = call(
                diag_kernel,
                [((4, W, W), F32)],
                (place, columns_t, *outs),
                [SMEM] + [VMEM] * 5,
                [VMEM],
                flops=2 * ORDER * W * W,
            )
            terms = (columns_t, term)
    panel = ((NR, NC, RD, W), BF16)
    (green_panel,) = call(
        functools.partial(final_kernel, 0),
        [panel],
        (place, *parts[:4]),
        [SMEM] + [ANY] * 4,
        [ANY],
        [dma((16,))],
    )
    green_panel, green_diag = call(
        functools.partial(final_kernel, 1),
        [panel, ((W, W), F32)],
        (place, pivot_inverse.reshape(W, W), *parts[4:], green_panel),
        [SMEM, VMEM] + [ANY] * 5,
        [ANY, VMEM],
        [pltpu.VMEM((4, W, W), BF16), dma((20,))],
        aliases=((6, 0),),
    )
    return green_panel.reshape(ORDER, 1, W), green_diag.reshape(1, W, W)


def solution(mesh):
    placed = (
        P("pole", "col", None, "row"),
        P(("row", "col"), "pole", None),
        P(),
        P(("row", "col"), "pole", None),
    )
    return jax.shard_map(
        local,
        mesh=mesh,
        in_specs=placed,
        out_specs=(P("pole", ("row", "col"), None), P(("row", "col"), "pole", None)),
        check_vma=False,
    )
```

```python
import functools

import jax
import jax.numpy as jnp
from jax import lax
from jax.experimental import pallas as pl
from jax.experimental.pallas import tpu as pltpu
from jax.sharding import PartitionSpec as P

BF16 = jnp.bfloat16
F32 = jnp.float32
SMEM = pl.BlockSpec(memory_space=pltpu.SMEM)
VMEM = pl.BlockSpec(memory_space=pltpu.VMEM)
ANY = pl.BlockSpec(memory_space=pl.ANY)

W = 128
RD = 192
CH = 2 * RD
NR = 4
NY = 4
NC = 8
SPAN = NC * RD
HALF = NR * RD
ORDER = NR * NC * RD
UP = 1


def run_copies(copies):
    for copy in copies:
        copy.start()
    for copy in copies:
        copy.wait()


def call(
    kernel, outs, ins, specs, out_specs, scratch=(), flops=0, bytes_accessed=1024, aliases=()
):
    return pl.pallas_call(
        kernel,
        out_shape=[jax.ShapeDtypeStruct(s, d) for s, d in outs],
        in_specs=specs,
        out_specs=out_specs,
        scratch_shapes=list(scratch),
        input_output_aliases=dict(aliases),
        compiler_params=pltpu.CompilerParams(vmem_limit_bytes=24 * 1024 * 1024),
        cost_estimate=pl.CostEstimate(
            flops=flops, bytes_accessed=bytes_accessed, transcendentals=0
        ),
    )(*ins)


def step_of(r, group, core):
    return lax.rem(r + 3 - group, 4) if core == UP else lax.rem(group + 3 - r, 4)


def along(index, count, core):
    return lax.rem(index + jnp.where(core == UP, count, 4 - count), 4)


def prep_kernel(place, pattern, panel, mine0, theirs0, mine, theirs, turned, sems):
    r, k, position = place[0], place[2], place[3]
    for group in range(NR):
        for part in range(3):
            block = lax.div(position * 3 + part, 2)
            for piece in range(2):
                rows = pl.ds(part * 64 + piece * 32, 32)
                value = jnp.swapaxes(
                    panel[rows, group * 8 : group * 8 + 8, :].astype(F32), 0, 1
                )
                for q in range(NY):
                    for parity in range(2):
                        keep = pattern[group * 8 + q * 2 + parity, block].astype(F32)
                        turned[lax.rem(parity + k, 2), step_of(r, group, parity), q, rows, :] = (
                            value[q * 2 + parity] * keep
                        ).astype(BF16)
    run_copies(
        [
            pltpu.make_async_copy(turned.at[who, part], out, sems.at[i])
            for i, (who, part, out) in enumerate(
                (
                    (1, 0, theirs0),
                    (0, 0, mine0),
                    (1, slice(1, 4), theirs),
                    (0, slice(1, 4), mine),
                )
            )
        ]
    )


def first_chunk_kernel(place, mine, got, after, chunk, sems):
    k = place[2]
    run_copies(
        [
            pltpu.make_async_copy(source, chunk.at[:, half], sems.at[i])
            for i, (source, half) in enumerate(((mine, k), (got, 1 - k)))
        ]
    )


def chunks_kernel(place, mine, got, after, c1, c2, c3, sems):
    k = place[2]
    copies = []
    for source, half in ((mine, k), (got, 1 - k)):
        for i, chunk in enumerate((c1, c2, c3)):
            copies.append(
                pltpu.make_async_copy(source.at[i], chunk.at[:, half], sems.at[len(copies)])
            )
    run_copies(copies)


def after_kernel(value, first, second, out, sems):
    run_copies([pltpu.make_async_copy(value, out, sems.at[0])])


def load_panel(place, pieces, panel, sems):
    y, k = place[1], place[2]
    copies = []
    for hop, source in enumerate(pieces):
        rows = pl.ds(pl.multiple_of(along(y, 4 - hop, k) * CH, CH), CH)
        copies.append(pltpu.make_async_copy(source, panel.at[:, rows, :], sems.at[hop]))
    run_copies(copies)


def product_kernel(summed, place, green, *rest):
    pieces, rest = rest[:4], rest[4:]
    acc, (out, panel, sems) = rest[:summed], rest[-3:]
    load_panel(place, pieces, panel, sems)
    for h in range(2):
        both = jnp.concatenate([panel[2 * h], panel[2 * h + 1]], axis=1)
        value = jnp.dot(green[...], both, preferred_element_type=F32)
        for i in range(2):
            part = value[:, i * W : (i + 1) * W]
            if summed:
                part = part + acc[0][2 * h + i].astype(F32)
            out[2 * h + i] = part.astype(BF16)


def product(place, green, pieces, acc, after=()):
    (out,) = call(
        functools.partial(product_kernel, len(acc)),
        [((NY, HALF, W), BF16)],
        (place, green, *pieces, *acc, *after),
        [SMEM, VMEM] + [ANY] * 4 + [VMEM] * len(acc) + [ANY] * len(after),
        [VMEM],
        [pltpu.VMEM((NY, SPAN, W), BF16), pltpu.SemaphoreType.DMA((4,))],
    )
    return out


def last_kernel(half, place, pattern, green, *rest):
    pieces, acc, rest = rest[:4], rest[4], rest[5:]
    if half:
        columns_t, terms, opposite, rest = rest[0], rest[1], rest[2], rest[5:]
    outs, (panel, sems, *own) = rest[:4], rest[4:]
    r, y, k = place[0], place[1], place[2]
    if half:
        first = pltpu.make_async_copy(opposite, outs[2].at[HALF + W :], own[0].at[0])
        first.start()
    load_panel(place, pieces, panel, sems)
    c = y * 2 + (k if half == 0 else 1 - k)
    for h in range(2):
        order = [lax.rem(y + 2 * h + i, 4) for i in range(2)]
        both = jnp.concatenate([panel[order[0]], panel[order[1]]], axis=1)
        value = jnp.dot(green[...], both, preferred_element_type=F32)
        for i, q in enumerate(order):
            number = r * 8 + q * 2 + k
            out = outs[2 * h + i]
            for j in range(NR):
                for piece in range(3):
                    keep = -pattern[number, lax.div((j * 8 + c) * 3 + piece, 2)].astype(F32)
                    start = j * RD + piece * 64
                    rows = slice(start, start + 64)
                    part = value[rows, i * W : (i + 1) * W] + acc[q, rows, :].astype(F32)
                    out[rows, :] = (part * keep).astype(BF16)
            if half:
                term = jnp.dot(columns_t[1, q], out[0:HALF, :], preferred_element_type=F32)
                out[HALF : HALF + W, :] = (terms[2 * h + i] - term).astype(BF16)
    if half:
        first.wait()


def diag_kernel(place, columns_t, *rest):
    ended, out = rest[:4], rest[4]
    y = place[1]
    for d in range(4):
        q = lax.rem(y + d, 4)
        out[d] = -jnp.dot(columns_t[0, q], ended[d][...], preferred_element_type=F32)


def columns_kernel(place, x0, x1, x2, x3, out, columns, sems):
    r, k = place[0], place[2]
    run_copies(
        [
            pltpu.make_async_copy(source, columns.at[along(r, 1 + s, k)], sems.at[s])
            for s, source in enumerate((x0, x1, x2, x3))
        ]
    )
    for half in range(2):
        parity = k if half == 0 else 1 - k
        for q in range(NY):
            out[half, q] = columns[:, q, parity].reshape(HALF, W).T


def final_kernel(place, pivot, *rest):
    parts, (panel, diag, terms, sems) = rest[:7], rest[7:]
    y, k = place[1], place[2]
    sources = [
        (parts[0], 0, 0, 0),
        (parts[1], 0, 0, 1),
        (parts[2], 0, 0, 3),
        (parts[5], HALF + W, 0, 2),
        (parts[3], 0, 1, 0),
        (parts[4], 0, 1, 1),
        (parts[5], 0, 1, 2),
        (parts[6], 0, 1, 3),
    ]
    copies, last = [], []
    for source, start, half, d in sources:
        c = lax.rem(y + 4 - d, 4) * 2 + (k if half == 0 else 1 - k)
        for j in range(NR):
            rows = source.at[start + j * RD : start + (j + 1) * RD]
            copies.append(pltpu.make_async_copy(rows, panel.at[j, c], sems.at[len(copies)]))
        if half:
            rows = source.at[HALF : HALF + W]
            last.append(pltpu.make_async_copy(rows, terms.at[d], sems.at[NR * NC + d]))
    for copy in last + copies:
        copy.start()
    for copy in last:
        copy.wait()
    total = pivot[...]
    for d in range(4):
        total += terms[d].astype(F32)
    diag[...] = total
    for copy in copies:
        copy.wait()


def local(green_blocks, lower_panel, pattern, pivot_inverse):
    r = lax.axis_index("row")
    col = lax.axis_index("col")
    place = jnp.stack([r, col // 2, col % 2, r * 8 + col]).astype(jnp.int32)
    dma = pltpu.SemaphoreType.DMA

    def sib(v):
        return lax.ppermute(v, "col", [(c, c ^ 1) for c in range(8)])

    def over_y(v, d):
        return lax.ppermute(v, "col", [(c, (c + 2 * d) % 8) for c in range(8)])

    def ring_y(v, d=1):
        pairs = [(c, (c + (2 * d if c % 2 == UP else -2 * d)) % 8) for c in range(8)]
        return lax.ppermute(v, "col", pairs)

    def ring_x(v, d=1):
        pairs = [(i, (i + (8 * d if i % 2 == UP else -8 * d)) % 32) for i in range(32)]
        return lax.ppermute(v, ("row", "col"), pairs)

    pattern = pattern.T
    small, large = ((NY, RD, W), BF16), ((3, NY, RD, W), BF16)
    mine0, theirs0, mine, theirs = call(
        prep_kernel,
        [small, small, large, large],
        (place, pattern, lower_panel),
        [SMEM, SMEM, VMEM],
        [ANY] * 4,
        [pltpu.VMEM((2, NR, NY, RD, W), BF16), dma((4,))],
    )
    got0 = sib(theirs0)
    got = sib(theirs)
    green_own = green_blocks.reshape(HALF, SPAN)
    greens = (green_own, sib(green_own))

    chunk = ((NY, 2, RD, W), BF16)
    (chunk0,) = call(
        first_chunk_kernel,
        [chunk],
        (place, mine0, got0, greens[1]),
        [SMEM] + [ANY] * 3,
        [ANY],
        [dma((2,))],
    )
    chunks = (chunk0,) + tuple(
        call(
            chunks_kernel,
            [chunk] * 3,
            (place, mine, got, chunk0),
            [SMEM] + [ANY] * 3,
            [ANY] * 3,
            [dma((6,))],
        )
    )
    columns = [ring_x(chunks[0], 3), None, ring_x(chunks[2], 1), chunks[3]]
    (sent,) = call(
        after_kernel,
        [chunk],
        (chunks[1], columns[0], columns[2]),
        [ANY] * 3,
        [ANY],
        [dma((1,))],
    )
    columns[1] = ring_x(sent, 2)
    (columns_t,) = call(
        columns_kernel,
        [((2, NY, W, HALF), BF16)],
        (place, *columns),
        [SMEM] + [ANY] * 4,
        [VMEM],
        [pltpu.VMEM((NR, NY, 2, RD, W), BF16), dma((4,))],
    )

    pieces = []
    for s in range(NR):
        sent = own = chunks[s].reshape(NY, CH, W)
        if s:
            (sent,) = call(
                after_kernel,
                [((NY, CH, W), BF16)],
                (own, *near),
                [ANY] * 3,
                [ANY],
                [dma((1,))],
            )
        near = (ring_y(sent), ring_y(sent, -1))
        pieces.append((own, near[0], ring_y(near[0]), near[1]))

    before = {
        (0, 0): (columns[0], columns[2]),
        (0, 1): (pieces[1][1], pieces[1][3], columns[1]),
        (1, 0): (columns_t,),
        (1, 1): (pieces[2][1], pieces[2][3]),
        (2, 0): (),
        (2, 1): (pieces[3][1], pieces[3][3]),
    }
    acc = [(), ()]
    for s in range(NR - 1):
        for half in range(2):
            after = before[s, half]
            if s == 0 and half:
                after += (out,)
            out = product(place, greens[half], pieces[s], acc[half], after)
            acc[half] = (ring_x(out),)
    parts, terms, last_after = [], (), ()
    for half in range(2):
        rows = [HALF + W * half] * 4
        rows[2] += HALF * half
        outs = call(
            functools.partial(last_kernel, half),
            [((n, W), BF16) for n in rows],
            (place, pattern, greens[half], *pieces[3], *acc[half], *terms, *last_after),
            [SMEM, SMEM, VMEM]
            + [ANY] * 4
            + [VMEM] * (1 + len(terms))
            + [ANY] * len(last_after),
            [VMEM] * 4,
            [pltpu.VMEM((NY, SPAN, W), BF16), dma((4,))] + [dma((1,))] * half,
        )
        parts.append(outs[0])
        for d in (1, 2, 3) if half else (1, 3):
            parts.append(over_y(outs[d], d))
        if half == 0:
            (term,) = call(
                diag_kernel,
                [((4, W, W), F32)],
                (place, columns_t, *outs),
                [SMEM] + [VMEM] * 5,
                [VMEM],
            )
            terms = (columns_t, term)
            last_after = (outs[2], parts[1], parts[2])
    green_panel, green_diag = call(
        final_kernel,
        [((NR, NC, RD, W), BF16), ((W, W), F32)],
        (place, pivot_inverse.reshape(W, W), *parts),
        [SMEM, VMEM] + [ANY] * 7,
        [ANY, VMEM],
        [pltpu.VMEM((4, W, W), BF16), dma((36,))],
    )
    return green_panel.reshape(ORDER, 1, W), green_diag.reshape(1, W, W)


def solution(mesh):
    placed = (
        P("pole", "col", None, "row"),
        P(("row", "col"), "pole", None),
        P(),
        P(("row", "col"), "pole", None),
    )
    return jax.shard_map(
        local,
        mesh=mesh,
        in_specs=placed,
        out_specs=(P("pole", ("row", "col"), None), P(("row", "col"), "pole", None)),
        check_vma=False,
    )
```

```python
import functools

import jax
import jax.numpy as jnp
from jax import lax
from jax.experimental import pallas as pl
from jax.experimental.pallas import tpu as pltpu
from jax.sharding import PartitionSpec as P

BF16 = jnp.bfloat16
F32 = jnp.float32
SMEM = pl.BlockSpec(memory_space=pltpu.SMEM)
VMEM = pl.BlockSpec(memory_space=pltpu.VMEM)
ANY = pl.BlockSpec(memory_space=pl.ANY)

W = 128
RD = 192
CH = 2 * RD
NR = 4
NY = 4
NC = 8
SPAN = NC * RD
HALF = NR * RD
ORDER = NR * NC * RD
UP = 1


def run_copies(copies):
    for copy in copies:
        copy.start()
    for copy in copies:
        copy.wait()


def call(
    kernel, outs, ins, specs, out_specs, scratch=(), flops=0, bytes_accessed=1024, aliases=()
):
    return pl.pallas_call(
        kernel,
        out_shape=[jax.ShapeDtypeStruct(s, d) for s, d in outs],
        in_specs=specs,
        out_specs=out_specs,
        scratch_shapes=list(scratch),
        input_output_aliases=dict(aliases),
        compiler_params=pltpu.CompilerParams(vmem_limit_bytes=24 * 1024 * 1024),
        cost_estimate=pl.CostEstimate(
            flops=flops, bytes_accessed=bytes_accessed, transcendentals=0
        ),
    )(*ins)


def step_of(r, group, core):
    return lax.rem(r + 3 - group, 4) if core == UP else lax.rem(group + 3 - r, 4)


def along(index, count, core):
    return lax.rem(index + jnp.where(core == UP, count, 4 - count), 4)


def prep_kernel(place, pattern, panel, mine0, theirs0, mine, theirs, turned, sems):
    r, k, position = place[0], place[2], place[3]
    for group in range(NR):
        for part in range(3):
            block = lax.div(position * 3 + part, 2)
            for piece in range(2):
                rows = pl.ds(part * 64 + piece * 32, 32)
                value = jnp.swapaxes(
                    panel[rows, group * 8 : group * 8 + 8, :].astype(F32), 0, 1
                )
                for q in range(NY):
                    for parity in range(2):
                        keep = pattern[group * 8 + q * 2 + parity, block].astype(F32)
                        turned[lax.rem(parity + k, 2), step_of(r, group, parity), q, rows, :] = (
                            value[q * 2 + parity] * keep
                        ).astype(BF16)
    run_copies(
        [
            pltpu.make_async_copy(turned.at[who, part], out, sems.at[i])
            for i, (who, part, out) in enumerate(
                (
                    (1, 0, theirs0),
                    (0, 0, mine0),
                    (1, slice(1, 4), theirs),
                    (0, slice(1, 4), mine),
                )
            )
        ]
    )


def first_chunk_kernel(place, mine, got, after, chunk, sems):
    k = place[2]
    run_copies(
        [
            pltpu.make_async_copy(source, chunk.at[:, half], sems.at[i])
            for i, (source, half) in enumerate(((mine, k), (got, 1 - k)))
        ]
    )


def chunks_kernel(place, mine, got, after, c1, c2, c3, sems):
    k = place[2]
    copies = []
    for source, half in ((mine, k), (got, 1 - k)):
        for i, chunk in enumerate((c1, c2, c3)):
            copies.append(
                pltpu.make_async_copy(source.at[i], chunk.at[:, half], sems.at[len(copies)])
            )
    run_copies(copies)


def after_kernel(value, *rest):
    out, sems = rest[-2:]
    run_copies([pltpu.make_async_copy(value, out, sems.at[0])])


def turn_kernel(place, own, sib, own_out, sib_out, sems):
    y, k = place[1], place[2]
    copies = []
    for source, target in ((own, own_out), (sib, sib_out)):
        for hop in range(NY):
            columns = pl.ds(pl.multiple_of(along(y, 4 - hop, k) * CH, CH), CH)
            copies.append(
                pltpu.make_async_copy(
                    source.at[:, columns],
                    target.at[:, hop * CH : (hop + 1) * CH],
                    sems.at[len(copies)],
                )
            )
    run_copies(copies)


def multiply(green, pieces, first, second):
    both = jnp.concatenate(
        [jnp.concatenate([p[first], p[second]], axis=1) for p in pieces], axis=0
    )
    return jnp.dot(green[...], both, preferred_element_type=F32)


def product_kernel(summed, green, *rest):
    pieces, rest = rest[:4], rest[4:]
    acc, out = rest[:summed], rest[-1]
    for h in range(2):
        value = multiply(green, pieces, 2 * h, 2 * h + 1)
        for i in range(2):
            part = value[:, i * W : (i + 1) * W]
            if summed:
                part = part + acc[0][2 * h + i].astype(F32)
            out[2 * h + i] = part.astype(BF16)


def product(green, pieces, acc, after=()):
    (out,) = call(
        functools.partial(product_kernel, len(acc)),
        [((NY, HALF, W), BF16)],
        (green, *pieces, *acc, *after),
        [VMEM] * (5 + len(acc)) + [ANY] * len(after),
        [VMEM],
    )
    return out


def last_kernel(half, place, pattern, green, *rest):
    pieces, acc, rest = rest[:4], rest[4], rest[5:]
    if half:
        columns_t, terms, opposite, rest = rest[0], rest[1], rest[2], rest[5:]
    outs, own = rest[:4], rest[4:]
    r, y, k = place[0], place[1], place[2]
    if half:
        first = pltpu.make_async_copy(opposite, outs[2].at[HALF + W :], own[0].at[0])
        first.start()
    c = y * 2 + (k if half == 0 else 1 - k)
    for h in range(2):
        order = [lax.rem(y + 2 * h + i, 4) for i in range(2)]
        value = multiply(green, pieces, *order)
        for i, q in enumerate(order):
            number = r * 8 + q * 2 + k
            out = outs[2 * h + i]
            for j in range(NR):
                for piece in range(3):
                    keep = -pattern[number, lax.div((j * 8 + c) * 3 + piece, 2)].astype(F32)
                    start = j * RD + piece * 64
                    rows = slice(start, start + 64)
                    part = value[rows, i * W : (i + 1) * W] + acc[q, rows, :].astype(F32)
                    out[rows, :] = (part * keep).astype(BF16)
        if half:
            left = jnp.concatenate([columns_t[1, q] for q in order], axis=0)
            right = jnp.concatenate([outs[2 * h + i][0:HALF, :] for i in range(2)], axis=1)
            term = jnp.dot(left, right, preferred_element_type=F32)
            for i in range(2):
                block = slice(i * W, (i + 1) * W)
                outs[2 * h + i][HALF : HALF + W, :] = (
                    terms[2 * h + i] - term[block, block]
                ).astype(BF16)
    if half:
        first.wait()


def diag_kernel(place, columns_t, *rest):
    ended, out = rest[:4], rest[4]
    y = place[1]
    for d in range(4):
        q = lax.rem(y + d, 4)
        out[d] = -jnp.dot(columns_t[0, q], ended[d][...], preferred_element_type=F32)


def columns_kernel(place, x0, x1, x2, x3, out, columns, sems):
    r, k = place[0], place[2]
    run_copies(
        [
            pltpu.make_async_copy(source, columns.at[along(r, 1 + s, k)], sems.at[s])
            for s, source in enumerate((x0, x1, x2, x3))
        ]
    )
    for half in range(2):
        parity = k if half == 0 else 1 - k
        for q in range(NY):
            out[half, q] = columns[:, q, parity].reshape(HALF, W).T


def final_kernel(place, pivot, *rest):
    parts, (panel, diag, sems) = rest[:7], rest[7:]
    y, k = place[1], place[2]
    sources = [
        (parts[0], 0, 0, 0),
        (parts[1], 0, 0, 1),
        (parts[2], 0, 0, 3),
        (parts[5], HALF + W, 0, 2),
        (parts[3], 0, 1, 0),
        (parts[4], 0, 1, 1),
        (parts[5], 0, 1, 2),
        (parts[6], 0, 1, 3),
    ]
    copies = []
    for source, start, half, d in sources:
        c = lax.rem(y + 4 - d, 4) * 2 + (k if half == 0 else 1 - k)
        for j in range(NR):
            rows = source.at[start + j * RD : start + (j + 1) * RD]
            copies.append(pltpu.make_async_copy(rows, panel.at[j, c], sems.at[len(copies)]))
    for copy in copies:
        copy.start()
    total = pivot[...]
    for source in parts[3:]:
        total += source[HALF : HALF + W, :].astype(F32)
    diag[...] = total
    for copy in copies:
        copy.wait()


def local(green_blocks, lower_panel, pattern, pivot_inverse):
    r = lax.axis_index("row")
    col = lax.axis_index("col")
    place = jnp.stack([r, col // 2, col % 2, r * 8 + col]).astype(jnp.int32)
    dma = pltpu.SemaphoreType.DMA

    def sib(v):
        return lax.ppermute(v, "col", [(c, c ^ 1) for c in range(8)])

    def over_y(v, d):
        return lax.ppermute(v, "col", [(c, (c + 2 * d) % 8) for c in range(8)])

    def ring_y(v, d=1):
        pairs = [(c, (c + (2 * d if c % 2 == UP else -2 * d)) % 8) for c in range(8)]
        return lax.ppermute(v, "col", pairs)

    def ring_x(v, d=1):
        pairs = [(i, (i + (8 * d if i % 2 == UP else -8 * d)) % 32) for i in range(32)]
        return lax.ppermute(v, ("row", "col"), pairs)

    pattern = pattern.T
    small, large = ((NY, RD, W), BF16), ((3, NY, RD, W), BF16)
    mine0, theirs0, mine, theirs = call(
        prep_kernel,
        [small, small, large, large],
        (place, pattern, lower_panel),
        [SMEM, SMEM, VMEM],
        [ANY] * 4,
        [pltpu.VMEM((2, NR, NY, RD, W), BF16), dma((4,))],
    )
    got0 = sib(theirs0)
    got = sib(theirs)
    green_own = green_blocks.reshape(HALF, SPAN)
    greens = (green_own, sib(green_own))

    chunk = ((NY, 2, RD, W), BF16)
    (chunk0,) = call(
        first_chunk_kernel,
        [chunk],
        (place, mine0, got0, greens[1]),
        [SMEM] + [ANY] * 3,
        [ANY],
        [dma((2,))],
    )
    chunks = (chunk0,) + tuple(
        call(
            chunks_kernel,
            [chunk] * 3,
            (place, mine, got, chunk0),
            [SMEM] + [ANY] * 3,
            [ANY] * 3,
            [dma((6,))],
        )
    )
    columns = [ring_x(chunks[0], 3), None, ring_x(chunks[2], 1), chunks[3]]
    turned = call(
        turn_kernel,
        [((HALF, SPAN), BF16)] * 2,
        (place, *greens),
        [SMEM, ANY, ANY],
        [ANY] * 2,
        [dma((8,))],
    )
    (sent,) = call(
        after_kernel,
        [chunk],
        (chunks[1], columns[0], columns[2], *turned),
        [ANY] * 5,
        [ANY],
        [dma((1,))],
    )
    columns[1] = ring_x(sent, 2)
    (columns_t,) = call(
        columns_kernel,
        [((2, NY, W, HALF), BF16)],
        (place, *columns),
        [SMEM] + [ANY] * 4,
        [VMEM],
        [pltpu.VMEM((NR, NY, 2, RD, W), BF16), dma((4,))],
    )

    pieces = []
    for s in range(NR):
        sent = own = chunks[s].reshape(NY, CH, W)
        if s:
            (sent,) = call(
                after_kernel,
                [((NY, CH, W), BF16)],
                (own, *near),
                [ANY] * 3,
                [ANY],
                [dma((1,))],
            )
        near = (ring_y(sent), ring_y(sent, -1))
        pieces.append((own, near[0], ring_y(near[0]), near[1]))

    before = {
        (0, 0): (columns[0], columns[2]),
        (0, 1): (pieces[1][1], pieces[1][3], columns[1]),
        (1, 0): (columns_t,),
        (1, 1): (pieces[2][1], pieces[2][3]),
        (2, 0): (),
        (2, 1): (pieces[3][1], pieces[3][3]),
    }
    acc = [(), ()]
    for s in range(NR - 1):
        for half in range(2):
            after = before[s, half]
            if s == 0 and half:
                after += (out,)
            out = product(turned[half], pieces[s], acc[half], after)
            acc[half] = (ring_x(out),)
    parts, terms, last_after = [], (), ()
    for half in range(2):
        rows = [HALF + W * half] * 4
        rows[2] += HALF * half
        outs = call(
            functools.partial(last_kernel, half),
            [((n, W), BF16) for n in rows],
            (place, pattern, turned[half], *pieces[3], *acc[half], *terms, *last_after),
            [SMEM, SMEM, VMEM]
            + [VMEM] * (5 + len(terms))
            + [ANY] * len(last_after),
            [VMEM] * 4,
            [dma((1,))] * half,
        )
        parts.append(outs[0])
        for d in (1, 2, 3) if half else (1, 3):
            parts.append(over_y(outs[d], d))
        if half == 0:
            (term,) = call(
                diag_kernel,
                [((4, W, W), F32)],
                (place, columns_t, *outs),
                [SMEM] + [VMEM] * 5,
                [VMEM],
            )
            terms = (columns_t, term)
            last_after = (outs[2], parts[1], parts[2])
    green_panel, green_diag = call(
        final_kernel,
        [((NR, NC, RD, W), BF16), ((W, W), F32)],
        (place, pivot_inverse.reshape(W, W), *parts),
        [SMEM, VMEM] + [ANY] * 3 + [VMEM] * 4,
        [ANY, VMEM],
        [dma((32,))],
    )
    return green_panel.reshape(ORDER, 1, W), green_diag.reshape(1, W, W)


def solution(mesh):
    placed = (
        P("pole", "col", None, "row"),
        P(("row", "col"), "pole", None),
        P(),
        P(("row", "col"), "pole", None),
    )
    return jax.shard_map(
        local,
        mesh=mesh,
        in_specs=placed,
        out_specs=(P("pole", ("row", "col"), None), P(("row", "col"), "pole", None)),
        check_vma=False,
    )
```

```python
import functools

import jax
import jax.numpy as jnp
from jax import lax
from jax.experimental import pallas as pl
from jax.experimental.pallas import tpu as pltpu
from jax.sharding import PartitionSpec as P

BF16 = jnp.bfloat16
F32 = jnp.float32
SMEM = pl.BlockSpec(memory_space=pltpu.SMEM)
VMEM = pl.BlockSpec(memory_space=pltpu.VMEM)
ANY = pl.BlockSpec(memory_space=pl.ANY)

W = 128
RD = 192
CH = 2 * RD
NR = 4
NY = 4
NC = 8
SPAN = NC * RD
HALF = NR * RD
ORDER = NR * NC * RD
UP = 1


def run_copies(copies):
    for copy in copies:
        copy.start()
    for copy in copies:
        copy.wait()


def call(
    kernel, outs, ins, specs, out_specs, scratch=(), flops=0, bytes_accessed=1024, aliases=()
):
    return pl.pallas_call(
        kernel,
        out_shape=[jax.ShapeDtypeStruct(s, d) for s, d in outs],
        in_specs=specs,
        out_specs=out_specs,
        scratch_shapes=list(scratch),
        input_output_aliases=dict(aliases),
        compiler_params=pltpu.CompilerParams(vmem_limit_bytes=24 * 1024 * 1024),
        cost_estimate=pl.CostEstimate(
            flops=flops, bytes_accessed=bytes_accessed, transcendentals=0
        ),
    )(*ins)


def step_of(r, group, core):
    return lax.rem(r + 3 - group, 4) if core == UP else lax.rem(group + 3 - r, 4)


def along(index, count, core):
    return lax.rem(index + jnp.where(core == UP, count, 4 - count), 4)


def prep_kernel(place, pattern, panel, mine0, theirs0, mine, theirs, turned, sems):
    r, k, position = place[0], place[2], place[3]
    for group in range(NR):
        for part in range(3):
            block = lax.div(position * 3 + part, 2)
            for piece in range(2):
                rows = pl.ds(part * 64 + piece * 32, 32)
                value = jnp.swapaxes(
                    panel[rows, group * 8 : group * 8 + 8, :].astype(F32), 0, 1
                )
                for q in range(NY):
                    for parity in range(2):
                        keep = pattern[group * 8 + q * 2 + parity, block].astype(F32)
                        turned[lax.rem(parity + k, 2), step_of(r, group, parity), q, rows, :] = (
                            value[q * 2 + parity] * keep
                        ).astype(BF16)
    run_copies(
        [
            pltpu.make_async_copy(turned.at[who, part], out, sems.at[i])
            for i, (who, part, out) in enumerate(
                (
                    (1, 0, theirs0),
                    (0, 0, mine0),
                    (1, slice(1, 4), theirs),
                    (0, slice(1, 4), mine),
                )
            )
        ]
    )


def first_chunk_kernel(place, mine, got, after, chunk, sems):
    k = place[2]
    run_copies(
        [
            pltpu.make_async_copy(source, chunk.at[:, half], sems.at[i])
            for i, (source, half) in enumerate(((mine, k), (got, 1 - k)))
        ]
    )


def chunks_kernel(place, mine, got, after, c1, c2, c3, sems):
    k = place[2]
    copies = []
    for source, half in ((mine, k), (got, 1 - k)):
        for i, chunk in enumerate((c1, c2, c3)):
            copies.append(
                pltpu.make_async_copy(source.at[i], chunk.at[:, half], sems.at[len(copies)])
            )
    run_copies(copies)


def after_kernel(value, *rest):
    out, sems = rest[-2:]
    run_copies([pltpu.make_async_copy(value, out, sems.at[0])])


def turn_kernel(place, own, sib, own_out, sib_out, sems):
    y, k = place[1], place[2]
    copies = []
    for source, target in ((own, own_out), (sib, sib_out)):
        for hop in range(NY):
            columns = pl.ds(pl.multiple_of(along(y, 4 - hop, k) * CH, CH), CH)
            copies.append(
                pltpu.make_async_copy(
                    source.at[:, columns],
                    target.at[:, hop * CH : (hop + 1) * CH],
                    sems.at[len(copies)],
                )
            )
    run_copies(copies)


def multiply(green, pieces, first, second):
    both = jnp.concatenate(
        [jnp.concatenate([p[first], p[second]], axis=1) for p in pieces], axis=0
    )
    return jnp.dot(green[...], both, preferred_element_type=F32)


def product_kernel(summed, green, *rest):
    pieces, rest = rest[:4], rest[4:]
    acc, out = rest[:summed], rest[-1]
    for h in range(2):
        value = multiply(green, pieces, 2 * h, 2 * h + 1)
        for i in range(2):
            part = value[:, i * W : (i + 1) * W]
            if summed:
                part = part + acc[0][2 * h + i].astype(F32)
            out[2 * h + i] = part.astype(BF16)


def product(green, pieces, acc, after=()):
    (out,) = call(
        functools.partial(product_kernel, len(acc)),
        [((NY, HALF, W), BF16)],
        (green, *pieces, *acc, *after),
        [VMEM] * (5 + len(acc)) + [ANY] * len(after),
        [VMEM],
    )
    return out


def last_kernel(half, place, pattern, green, *rest):
    pieces, acc, rest = rest[:4], rest[4], rest[5:]
    if half:
        columns_t, terms, opposite, rest = rest[0], rest[1], rest[2], rest[5:]
    outs, own = rest[:4], rest[4:]
    r, y, k = place[0], place[1], place[2]
    if half:
        first = pltpu.make_async_copy(opposite, outs[2].at[HALF + W :], own[0].at[0])
        first.start()
    c = y * 2 + (k if half == 0 else 1 - k)
    for h in range(2):
        order = [lax.rem(y + 2 * h + i, 4) for i in range(2)]
        value = multiply(green, pieces, *order)
        for i, q in enumerate(order):
            number = r * 8 + q * 2 + k
            out = outs[2 * h + i]
            for j in range(NR):
                for piece in range(3):
                    keep = -pattern[number, lax.div((j * 8 + c) * 3 + piece, 2)].astype(F32)
                    start = j * RD + piece * 64
                    rows = slice(start, start + 64)
                    part = value[rows, i * W : (i + 1) * W] + acc[q, rows, :].astype(F32)
                    out[rows, :] = (part * keep).astype(BF16)
    if half:
        for h in range(2):
            order = [lax.rem(y + 2 * h + i, 4) for i in range(2)]
            left = jnp.concatenate([columns_t[1, q] for q in order], axis=0)
            right = jnp.concatenate([outs[2 * h + i][0:HALF, :] for i in range(2)], axis=1)
            term = jnp.dot(left, right, preferred_element_type=F32)
            for i in range(2):
                block = slice(i * W, (i + 1) * W)
                outs[2 * h + i][HALF : HALF + W, :] = (
                    terms[2 * h + i] - term[block, block]
                ).astype(BF16)
        first.wait()


def diag_kernel(place, columns_t, *rest):
    ended, out = rest[:4], rest[4]
    y = place[1]
    for d in range(4):
        q = lax.rem(y + d, 4)
        out[d] = -jnp.dot(columns_t[0, q], ended[d][...], preferred_element_type=F32)


def columns_kernel(place, x0, x1, x2, x3, out, columns, sems):
    r, k = place[0], place[2]
    run_copies(
        [
            pltpu.make_async_copy(source, columns.at[along(r, 1 + s, k)], sems.at[s])
            for s, source in enumerate((x0, x1, x2, x3))
        ]
    )
    for half in range(2):
        parity = k if half == 0 else 1 - k
        for q in range(NY):
            out[half, q] = columns[:, q, parity].reshape(HALF, W).T


def final_kernel(place, pivot, *rest):
    parts, (panel, diag, sems) = rest[:7], rest[7:]
    y, k = place[1], place[2]
    sources = [
        (parts[0], 0, 0, 0),
        (parts[1], 0, 0, 1),
        (parts[2], 0, 0, 3),
        (parts[5], HALF + W, 0, 2),
        (parts[3], 0, 1, 0),
        (parts[4], 0, 1, 1),
        (parts[5], 0, 1, 2),
        (parts[6], 0, 1, 3),
    ]
    copies = []
    for source, start, half, d in sources:
        c = lax.rem(y + 4 - d, 4) * 2 + (k if half == 0 else 1 - k)
        for j in range(NR):
            rows = source.at[start + j * RD : start + (j + 1) * RD]
            copies.append(pltpu.make_async_copy(rows, panel.at[j, c], sems.at[len(copies)]))
    for copy in copies:
        copy.start()
    total = pivot[...]
    for source in parts[3:]:
        total += source[HALF : HALF + W, :].astype(F32)
    diag[...] = total
    for copy in copies:
        copy.wait()


def local(green_blocks, lower_panel, pattern, pivot_inverse):
    r = lax.axis_index("row")
    col = lax.axis_index("col")
    place = jnp.stack([r, col // 2, col % 2, r * 8 + col]).astype(jnp.int32)
    dma = pltpu.SemaphoreType.DMA

    def sib(v):
        return lax.ppermute(v, "col", [(c, c ^ 1) for c in range(8)])

    def over_y(v, d):
        return lax.ppermute(v, "col", [(c, (c + 2 * d) % 8) for c in range(8)])

    def ring_y(v, d=1):
        pairs = [(c, (c + (2 * d if c % 2 == UP else -2 * d)) % 8) for c in range(8)]
        return lax.ppermute(v, "col", pairs)

    def ring_x(v, d=1):
        pairs = [(i, (i + (8 * d if i % 2 == UP else -8 * d)) % 32) for i in range(32)]
        return lax.ppermute(v, ("row", "col"), pairs)

    pattern = pattern.T
    small, large = ((NY, RD, W), BF16), ((3, NY, RD, W), BF16)
    mine0, theirs0, mine, theirs = call(
        prep_kernel,
        [small, small, large, large],
        (place, pattern, lower_panel),
        [SMEM, SMEM, VMEM],
        [ANY] * 4,
        [pltpu.VMEM((2, NR, NY, RD, W), BF16), dma((4,))],
    )
    got0 = sib(theirs0)
    got = sib(theirs)
    green_own = green_blocks.reshape(HALF, SPAN)
    greens = (green_own, sib(green_own))

    chunk = ((NY, 2, RD, W), BF16)
    (chunk0,) = call(
        first_chunk_kernel,
        [chunk],
        (place, mine0, got0, greens[1]),
        [SMEM] + [ANY] * 3,
        [ANY],
        [dma((2,))],
    )
    chunks = (chunk0,) + tuple(
        call(
            chunks_kernel,
            [chunk] * 3,
            (place, mine, got, chunk0),
            [SMEM] + [ANY] * 3,
            [ANY] * 3,
            [dma((6,))],
        )
    )
    columns = [ring_x(chunks[0], 3), None, ring_x(chunks[2], 1), chunks[3]]
    turned = call(
        turn_kernel,
        [((HALF, SPAN), BF16)] * 2,
        (place, *greens),
        [SMEM, ANY, ANY],
        [ANY] * 2,
        [dma((8,))],
    )
    (sent,) = call(
        after_kernel,
        [chunk],
        (chunks[1], columns[0], columns[2], *turned),
        [ANY] * 5,
        [ANY],
        [dma((1,))],
    )
    columns[1] = ring_x(sent, 2)
    (columns_t,) = call(
        columns_kernel,
        [((2, NY, W, HALF), BF16)],
        (place, *columns),
        [SMEM] + [ANY] * 4,
        [VMEM],
        [pltpu.VMEM((NR, NY, 2, RD, W), BF16), dma((4,))],
    )

    pieces = []
    for s in range(NR):
        sent = own = chunks[s].reshape(NY, CH, W)
        if s:
            (sent,) = call(
                after_kernel,
                [((NY, CH, W), BF16)],
                (own, *near),
                [ANY] * 3,
                [ANY],
                [dma((1,))],
            )
        near = (ring_y(sent), ring_y(sent, -1))
        pieces.append((own, near[0], ring_y(near[0]), near[1]))

    before = {
        (0, 0): (columns[0], columns[2]),
        (0, 1): (pieces[1][1], pieces[1][3], columns[1]),
        (1, 0): (columns_t,),
        (1, 1): (pieces[2][1], pieces[2][3]),
        (2, 0): (),
        (2, 1): (pieces[3][1], pieces[3][3]),
    }
    acc = [(), ()]
    for s in range(NR - 1):
        for half in range(2):
            after = before[s, half]
            if s == 0 and half:
                after += (out,)
            out = product(turned[half], pieces[s], acc[half], after)
            acc[half] = (ring_x(out),)
    parts, terms, last_after = [], (), ()
    for half in range(2):
        rows = [HALF + W * half] * 4
        rows[2] += HALF * half
        outs = call(
            functools.partial(last_kernel, half),
            [((n, W), BF16) for n in rows],
            (place, pattern, turned[half], *pieces[3], *acc[half], *terms, *last_after),
            [SMEM, SMEM, VMEM]
            + [VMEM] * (5 + len(terms))
            + [ANY] * len(last_after),
            [VMEM] * 4,
            [dma((1,))] * half,
        )
        parts.append(outs[0])
        for d in (1, 2, 3) if half else (1, 3):
            parts.append(over_y(outs[d], d))
        if half == 0:
            (term,) = call(
                diag_kernel,
                [((4, W, W), F32)],
                (place, columns_t, *outs),
                [SMEM] + [VMEM] * 5,
                [VMEM],
            )
            terms = (columns_t, term)
            last_after = (outs[2], parts[1], parts[2])
    green_panel, green_diag = call(
        final_kernel,
        [((NR, NC, RD, W), BF16), ((W, W), F32)],
        (place, pivot_inverse.reshape(W, W), *parts),
        [SMEM, VMEM] + [ANY] * 3 + [VMEM] * 4,
        [ANY, VMEM],
        [dma((32,))],
    )
    return green_panel.reshape(ORDER, 1, W), green_diag.reshape(1, W, W)


def solution(mesh):
    placed = (
        P("pole", "col", None, "row"),
        P(("row", "col"), "pole", None),
        P(),
        P(("row", "col"), "pole", None),
    )
    return jax.shard_map(
        local,
        mesh=mesh,
        in_specs=placed,
        out_specs=(P("pole", ("row", "col"), None), P(("row", "col"), "pole", None)),
        check_vma=False,
    )
```

```python
import functools

import jax
import jax.numpy as jnp
from jax import lax
from jax.experimental import pallas as pl
from jax.experimental.pallas import tpu as pltpu
from jax.sharding import PartitionSpec as P

BF16 = jnp.bfloat16
F32 = jnp.float32
SMEM = pl.BlockSpec(memory_space=pltpu.SMEM)
VMEM = pl.BlockSpec(memory_space=pltpu.VMEM)
ANY = pl.BlockSpec(memory_space=pl.ANY)

W = 128
RD = 192
CH = 2 * RD
NR = 4
NY = 4
NC = 8
SPAN = NC * RD
HALF = NR * RD
ORDER = NR * NC * RD
UP = 1


def run_copies(copies):
    for copy in copies:
        copy.start()
    for copy in copies:
        copy.wait()


def call(
    kernel, outs, ins, specs, out_specs, scratch=(), flops=0, bytes_accessed=1024, aliases=()
):
    return pl.pallas_call(
        kernel,
        out_shape=[jax.ShapeDtypeStruct(s, d) for s, d in outs],
        in_specs=specs,
        out_specs=out_specs,
        scratch_shapes=list(scratch),
        input_output_aliases=dict(aliases),
        compiler_params=pltpu.CompilerParams(vmem_limit_bytes=24 * 1024 * 1024),
        cost_estimate=pl.CostEstimate(
            flops=flops, bytes_accessed=bytes_accessed, transcendentals=0
        ),
    )(*ins)


def step_of(r, group, core):
    return lax.rem(r + 3 - group, 4) if core == UP else lax.rem(group + 3 - r, 4)


def along(index, count, core):
    return lax.rem(index + jnp.where(core == UP, count, 4 - count), 4)


def prep_kernel(place, pattern, panel, mine0, theirs0, mine, theirs, turned, sems):
    r, k, position = place[0], place[2], place[3]
    for group in range(NR):
        for part in range(3):
            block = lax.div(position * 3 + part, 2)
            for piece in range(2):
                rows = pl.ds(part * 64 + piece * 32, 32)
                value = jnp.swapaxes(
                    panel[rows, group * 8 : group * 8 + 8, :].astype(F32), 0, 1
                )
                for q in range(NY):
                    for parity in range(2):
                        keep = pattern[group * 8 + q * 2 + parity, block].astype(F32)
                        turned[lax.rem(parity + k, 2), step_of(r, group, parity), q, rows, :] = (
                            value[q * 2 + parity] * keep
                        ).astype(BF16)
    run_copies(
        [
            pltpu.make_async_copy(turned.at[who, part], out, sems.at[i])
            for i, (who, part, out) in enumerate(
                (
                    (1, 0, theirs0),
                    (0, 0, mine0),
                    (1, slice(1, 4), theirs),
                    (0, slice(1, 4), mine),
                )
            )
        ]
    )


def first_chunk_kernel(place, mine, got, after, chunk, sems):
    k = place[2]
    run_copies(
        [
            pltpu.make_async_copy(source, chunk.at[:, half], sems.at[i])
            for i, (source, half) in enumerate(((mine, k), (got, 1 - k)))
        ]
    )


def chunks_kernel(place, mine, got, after, c1, c2, c3, sems):
    k = place[2]
    copies = []
    for source, half in ((mine, k), (got, 1 - k)):
        for i, chunk in enumerate((c1, c2, c3)):
            copies.append(
                pltpu.make_async_copy(source.at[i], chunk.at[:, half], sems.at[len(copies)])
            )
    run_copies(copies)


def after_kernel(value, *rest):
    out, sems = rest[-2:]
    run_copies([pltpu.make_async_copy(value, out, sems.at[0])])


def turn_kernel(place, own, sib, own_out, sib_out, sems):
    y, k = place[1], place[2]
    copies = []
    for source, target in ((own, own_out), (sib, sib_out)):
        for hop in range(NY):
            columns = pl.ds(pl.multiple_of(along(y, 4 - hop, k) * CH, CH), CH)
            copies.append(
                pltpu.make_async_copy(
                    source.at[:, columns],
                    target.at[:, hop * CH : (hop + 1) * CH],
                    sems.at[len(copies)],
                )
            )
    run_copies(copies)


def multiply(green, pieces, first, second):
    both = jnp.concatenate(
        [jnp.concatenate([p[first], p[second]], axis=1) for p in pieces], axis=0
    )
    return jnp.dot(green[...], both, preferred_element_type=F32)


def product_kernel(summed, green, *rest):
    pieces, rest = rest[:4], rest[4:]
    acc, out = rest[:summed], rest[-1]
    for h in range(2):
        value = multiply(green, pieces, 2 * h, 2 * h + 1)
        for i in range(2):
            part = value[:, i * W : (i + 1) * W]
            if summed:
                part = part + acc[0][2 * h + i].astype(F32)
            out[2 * h + i] = part.astype(BF16)


def product(green, pieces, acc, after=()):
    (out,) = call(
        functools.partial(product_kernel, len(acc)),
        [((NY, HALF, W), BF16)],
        (green, *pieces, *acc, *after),
        [VMEM] * (5 + len(acc)) + [ANY] * len(after),
        [VMEM],
    )
    return out


def last_kernel(half, place, pattern, green, *rest):
    pieces, acc, rest = rest[:4], rest[4], rest[5:]
    if half:
        columns_t, terms, opposite, rest = rest[0], rest[1], rest[2], rest[5:]
    outs, own = rest[:4], rest[4:]
    r, y, k = place[0], place[1], place[2]
    if half:
        first = pltpu.make_async_copy(opposite, outs[2].at[HALF + W :], own[0].at[0])
        first.start()
    c = y * 2 + (k if half == 0 else 1 - k)
    for h in range(2):
        order = [lax.rem(y + 2 * h + i, 4) for i in range(2)]
        value = multiply(green, pieces, *order)
        for i, q in enumerate(order):
            number = r * 8 + q * 2 + k
            out = outs[2 * h + i]
            for j in range(NR):
                for piece in range(3):
                    keep = -pattern[number, lax.div((j * 8 + c) * 3 + piece, 2)].astype(F32)
                    start = j * RD + piece * 64
                    rows = slice(start, start + 64)
                    part = value[rows, i * W : (i + 1) * W] + acc[q, rows, :].astype(F32)
                    out[rows, :] = (part * keep).astype(BF16)
    if half:
        for h in range(2):
            order = [lax.rem(y + 2 * h + i, 4) for i in range(2)]
            left = jnp.concatenate([columns_t[1, q] for q in order], axis=0)
            right = jnp.concatenate([outs[2 * h + i][0:HALF, :] for i in range(2)], axis=1)
            term = jnp.dot(left, right, preferred_element_type=F32)
            for i in range(2):
                block = slice(i * W, (i + 1) * W)
                outs[2 * h + i][HALF : HALF + W, :] = (
                    terms[2 * h + i] - term[block, block]
                ).astype(BF16)
        first.wait()


def diag_kernel(place, columns_t, *rest):
    ended, out = rest[:4], rest[4]
    y = place[1]
    for d in range(4):
        q = lax.rem(y + d, 4)
        out[d] = -jnp.dot(columns_t[0, q], ended[d][...], preferred_element_type=F32)


def columns_kernel(place, x0, x1, x2, x3, out, columns, sems):
    r, k = place[0], place[2]
    run_copies(
        [
            pltpu.make_async_copy(source, columns.at[along(r, 1 + s, k)], sems.at[s])
            for s, source in enumerate((x0, x1, x2, x3))
        ]
    )
    for half in range(2):
        parity = k if half == 0 else 1 - k
        for q in range(NY):
            out[half, q] = columns[:, q, parity].reshape(HALF, W).T


def final_kernel(place, pivot, *rest):
    parts, (panel, diag, block, sems) = rest[:7], rest[7:]
    y, k = place[1], place[2]
    sources = [
        (parts[0], 0, 0, 0),
        (parts[1], 0, 0, 1),
        (parts[2], 0, 0, 3),
        (parts[5], HALF + W, 0, 2),
        (parts[3], 0, 1, 0),
        (parts[4], 0, 1, 1),
        (parts[5], 0, 1, 2),
        (parts[6], 0, 1, 3),
    ]
    copies = []
    for source, start, half, d in sources:
        c = lax.rem(y + 4 - d, 4) * 2 + (k if half == 0 else 1 - k)
        for j in range(NR):
            rows = source.at[start + j * RD : start + (j + 1) * RD]
            copies.append(pltpu.make_async_copy(rows, panel.at[j, c], sems.at[len(copies)]))
    for copy in copies:
        copy.start()
    total = pivot[...]
    for source in parts[3:]:
        total += source[HALF : HALF + W, :].astype(F32)
    block[...] = total
    copies.append(pltpu.make_async_copy(block, diag, sems.at[len(copies)]))
    copies[-1].start()
    for copy in copies:
        copy.wait()


def local(green_blocks, lower_panel, pattern, pivot_inverse):
    r = lax.axis_index("row")
    col = lax.axis_index("col")
    place = jnp.stack([r, col // 2, col % 2, r * 8 + col]).astype(jnp.int32)
    dma = pltpu.SemaphoreType.DMA

    def sib(v):
        return lax.ppermute(v, "col", [(c, c ^ 1) for c in range(8)])

    def over_y(v, d):
        return lax.ppermute(v, "col", [(c, (c + 2 * d) % 8) for c in range(8)])

    def ring_y(v, d=1):
        pairs = [(c, (c + (2 * d if c % 2 == UP else -2 * d)) % 8) for c in range(8)]
        return lax.ppermute(v, "col", pairs)

    def ring_x(v, d=1):
        pairs = [(i, (i + (8 * d if i % 2 == UP else -8 * d)) % 32) for i in range(32)]
        return lax.ppermute(v, ("row", "col"), pairs)

    pattern = pattern.T
    small, large = ((NY, RD, W), BF16), ((3, NY, RD, W), BF16)
    mine0, theirs0, mine, theirs = call(
        prep_kernel,
        [small, small, large, large],
        (place, pattern, lower_panel),
        [SMEM, SMEM, VMEM],
        [ANY] * 4,
        [pltpu.VMEM((2, NR, NY, RD, W), BF16), dma((4,))],
    )
    got0 = sib(theirs0)
    got = sib(theirs)
    green_own = green_blocks.reshape(HALF, SPAN)
    greens = (green_own, sib(green_own))

    chunk = ((NY, 2, RD, W), BF16)
    (chunk0,) = call(
        first_chunk_kernel,
        [chunk],
        (place, mine0, got0, greens[1]),
        [SMEM] + [ANY] * 3,
        [ANY],
        [dma((2,))],
    )
    chunks = (chunk0,) + tuple(
        call(
            chunks_kernel,
            [chunk] * 3,
            (place, mine, got, chunk0),
            [SMEM] + [ANY] * 3,
            [ANY] * 3,
            [dma((6,))],
        )
    )
    columns = [ring_x(chunks[0], 3), None, ring_x(chunks[2], 1), chunks[3]]
    turned = call(
        turn_kernel,
        [((HALF, SPAN), BF16)] * 2,
        (place, *greens),
        [SMEM, ANY, ANY],
        [ANY] * 2,
        [dma((8,))],
    )
    (sent,) = call(
        after_kernel,
        [chunk],
        (chunks[1], columns[0], columns[2], *turned),
        [ANY] * 5,
        [ANY],
        [dma((1,))],
    )
    columns[1] = ring_x(sent, 2)
    (columns_t,) = call(
        columns_kernel,
        [((2, NY, W, HALF), BF16)],
        (place, *columns),
        [SMEM] + [ANY] * 4,
        [VMEM],
        [pltpu.VMEM((NR, NY, 2, RD, W), BF16), dma((4,))],
    )

    pieces = []
    for s in range(NR):
        sent = own = chunks[s].reshape(NY, CH, W)
        if s:
            (sent,) = call(
                after_kernel,
                [((NY, CH, W), BF16)],
                (own, *near),
                [ANY] * 3,
                [ANY],
                [dma((1,))],
            )
        near = (ring_y(sent), ring_y(sent, -1))
        pieces.append((own, near[0], ring_y(near[0]), near[1]))

    before = {
        (0, 0): (columns[0], columns[2]),
        (0, 1): (pieces[1][1], pieces[1][3], columns[1]),
        (1, 0): (columns_t,),
        (1, 1): (pieces[2][1], pieces[2][3]),
        (2, 0): (),
        (2, 1): (pieces[3][1], pieces[3][3]),
    }
    acc = [(), ()]
    for s in range(NR - 1):
        for half in range(2):
            after = before[s, half]
            if s == 0 and half:
                after += (out,)
            out = product(turned[half], pieces[s], acc[half], after)
            acc[half] = (ring_x(out),)
    parts, terms, last_after = [], (), ()
    for half in range(2):
        rows = [HALF + W * half] * 4
        rows[2] += HALF * half
        outs = call(
            functools.partial(last_kernel, half),
            [((n, W), BF16) for n in rows],
            (place, pattern, turned[half], *pieces[3], *acc[half], *terms, *last_after),
            [SMEM, SMEM, VMEM]
            + [VMEM] * (5 + len(terms))
            + [ANY] * len(last_after),
            [VMEM] * 4,
            [dma((1,))] * half,
        )
        parts.append(outs[0])
        for d in (1, 2, 3) if half else (1, 3):
            parts.append(over_y(outs[d], d))
        if half == 0:
            (term,) = call(
                diag_kernel,
                [((4, W, W), F32)],
                (place, columns_t, *outs),
                [SMEM] + [VMEM] * 5,
                [VMEM],
            )
            terms = (columns_t, term)
            last_after = (outs[2], parts[1], parts[2])
    green_panel, green_diag = call(
        final_kernel,
        [((NR, NC, RD, W), BF16), ((W, W), F32)],
        (place, pivot_inverse.reshape(W, W), *parts),
        [SMEM, VMEM] + [ANY] * 3 + [VMEM] * 4,
        [ANY, ANY],
        [pltpu.VMEM((W, W), F32), dma((33,))],
    )
    return green_panel.reshape(ORDER, 1, W), green_diag.reshape(1, W, W)


def solution(mesh):
    placed = (
        P("pole", "col", None, "row"),
        P(("row", "col"), "pole", None),
        P(),
        P(("row", "col"), "pole", None),
    )
    return jax.shard_map(
        local,
        mesh=mesh,
        in_specs=placed,
        out_specs=(P("pole", ("row", "col"), None), P(("row", "col"), "pole", None)),
        check_vma=False,
    )
```
